512 devices in a mesh: wide: 32 (over x, y), narrow: 16 (over z, core).
Axes of the slice: x: 4, y: 8, z: 8, core: 2. Of those that a mesh axis runs over, the one named last changes fastest.
Arguments:
- hidden: bfloat16 [512, 4096], P('wide', 'narrow'), may hold values from -90 to 90
- head_weights: bfloat16 [4096, 303104], P(None, ('wide', 'narrow')), may hold values from -0.09375 to 0.09375
- token_ids: int32 [256], replicated, may hold values from 0 to 151551
- kl_weight: float32 [256], replicated, may hold values from 4 to 32
- advantage: float32 [256], replicated, may hold values from -12 to 12
Outputs:
- hidden_grad: float32 [4096, 512], P('narrow', 'wide')
- mixture_lse: float32 [256], replicated
- divergence: float32 [256], replicated
The draws below stay inside these ranges and needn't reach their ends.
All inputs are finite; a program needn't handle non-finite values.
Results may differ from the reference program's by a relative error of at most 0.012.
Values may be sent and summed in bfloat16 or wider, within the bound.
No kernel may reach another device: no remote copies, remote signals or barrier semaphores. Data moves between devices by JAX's collectives and lax.ppermute only.
A program may use at most 64 MiB of HBM per device.

```python
import math
import jax
import jax.numpy as jnp
import numpy as np

D = 4096
VOCAB = 151552
TOKENS = 256


def draw_hidden(key, part):
    key_rows, key_cols = jax.random.split(jax.random.fold_in(key, 11))
    base = jnp.clip(jax.random.normal(key_cols, (2 * TOKENS, D), jnp.float32), -6.0, 6.0)
    scale = jnp.exp(jax.random.uniform(key_rows, (2 * TOKENS, 1), jnp.float32, 0.0, 2.4849066))
    return (base * scale).astype(jnp.bfloat16)


def touch_ends(drawn, key, least, high):
    shape = drawn.shape
    spot = [jax.random.randint(jax.random.fold_in(key, axis), (), 0, shape[axis]) for axis in range(len(shape))]
    drawn = drawn.at[tuple(spot)].set(least)
    longest = shape.index(max(shape))
    spot[longest] = (spot[longest] + 1) % shape[longest]
    return drawn.at[tuple(spot)].set(high)


def block_scale(own_key, dims, shards, least, top_value):
    gain, own = 1.0, jax.random.fold_in(own_key, 6)
    for dim, blocks in shards:
        heights = jnp.exp(jax.random.uniform(jax.random.fold_in(own, dim), (blocks,), jnp.float32, least / len(shards), top_value / len(shards)))
        gain = gain * jnp.repeat(heights, dims[dim] // blocks).reshape([-1 if axis == dim else 1 for axis in range(len(dims))])
    return gain


def wide_ids(rng, extent, number_of, slope):
    portions = [min(1 << octave, number_of + 1 - (1 << octave)) * (1 << 20) // math.isqrt((1 << octave) ** slope) + 1 for octave in range((number_of + 1).bit_length()) if 1 << octave <= number_of]
    scale = 1 + sum(portions) // (1 << 30)
    listing = np.cumsum(np.array([max(1, weight // scale) for weight in portions]))
    lot = jax.random.randint(jax.random.fold_in(rng, 1), extent, 0, int(listing[len(portions) - 1]))
    start = jnp.left_shift(1, jnp.searchsorted(jnp.asarray(listing, jnp.int32), lot, side="right").astype(jnp.int32))
    grade = start - 1 + jax.random.randint(jax.random.fold_in(rng, 4), extent, 0, 1 << 30) % jnp.minimum(start, number_of + 1 - start)
    return jax.random.permutation(jax.random.fold_in(rng, 2), number_of)[grade].astype(jnp.int32)


def gaussian(stream_key, extent, deviation, bound, pieces=(), kind=jnp.bfloat16):
    values = jax.random.normal(stream_key, extent, jnp.float32) * deviation
    if len(pieces) > 0:
        values = block_scale(stream_key, extent, pieces, -0.22, 0.18) * values
    return jnp.clip(values, min=-bound, max=bound).astype(kind)


def setup_inputs(seed: int = 0) -> dict:
    arg_keys = jax.random.split(jax.random.key(seed), 6)
    return {
        "hidden": draw_hidden(jax.random.fold_in(arg_keys[5], 71), 0),
        "head_weights": gaussian(arg_keys[1], (D, 2 * VOCAB), D ** -0.5, 0.09375, ((1, 512),)),
        "token_ids": touch_ends(wide_ids(arg_keys[2], (TOKENS,), VOCAB, 2), jax.random.fold_in(arg_keys[2], 3), 0, VOCAB - 1).astype(jnp.int32),
        "kl_weight": jnp.clip(jnp.exp(jax.random.uniform(arg_keys[3], (TOKENS,), jnp.float32, math.log(4.0), math.log(32.0))), 4.0, 32.0),
        "advantage": gaussian(arg_keys[4], (TOKENS,), 4.0, 12.0, (), jnp.float32),
    }


BETA = 0.2


def reference(hidden, head_weights, token_ids, kl_weight, advantage):
    policy_logits = jnp.dot(hidden[:TOKENS], head_weights[:, :VOCAB], preferred_element_type=jnp.float32)
    ref_logits = jnp.dot(hidden[TOKENS:], head_weights[:, VOCAB:], preferred_element_type=jnp.float32)
    mixed_logits = (1.0 - BETA) * policy_logits + BETA * ref_logits
    policy_lse = jax.nn.logsumexp(policy_logits, axis=1)
    mixture_lse = jax.nn.logsumexp(mixed_logits, axis=1)
    policy_prob = jnp.exp(policy_logits - policy_lse[:, None])
    mixture_prob = jnp.exp(mixed_logits - mixture_lse[:, None])
    log_gap = policy_logits - policy_lse[:, None] - mixed_logits + mixture_lse[:, None]
    divergence = jnp.sum(policy_prob * log_gap, axis=1)
    chosen = (token_ids[:, None] == jnp.arange(VOCAB, dtype=jnp.int32)[None, :]).astype(jnp.float32)
    prob_shift = mixture_prob - policy_prob
    policy_dlogits = (kl_weight[:, None] * (policy_prob * (log_gap - divergence[:, None]) + (1.0 - BETA) * prob_shift) - advantage[:, None] * (chosen - policy_prob)).astype(jnp.bfloat16)
    ref_dlogits = (BETA * kl_weight[:, None] * prob_shift).astype(jnp.bfloat16)
    grad_policy = jnp.dot(head_weights[:, :VOCAB], policy_dlogits.T, preferred_element_type=jnp.float32)
    grad_reference = jnp.dot(head_weights[:, VOCAB:], ref_dlogits.T, preferred_element_type=jnp.float32)
    hidden_grad = jnp.concatenate([grad_policy, grad_reference], axis=1)
    return hidden_grad, mixture_lse, divergence
```

```python
import jax
import jax.numpy as jnp
from jax import lax
from jax.experimental import pallas as pl
from jax.experimental.pallas import tpu as pltpu
from jax.sharding import Mesh
from jax.sharding import PartitionSpec as P

HEAD, XLO, Y, Z, CORE = "head", "xlo", "y", "z", "core"
CHIPS = (XLO, Y, Z)
NARROW = (Z, CORE)
WIDE = (HEAD, XLO, Y)

BETA = 0.2
SWAP = [(0, 1), (1, 0)]
LANES = 128
STEP = 16
f32 = jnp.float32
bf16 = jnp.bfloat16
VMEM = pl.BlockSpec(memory_space=pltpu.VMEM)
SMEM = pl.BlockSpec(memory_space=pltpu.SMEM)
PARAMS = pltpu.CompilerParams(vmem_limit_bytes=40 << 20)


def logits_kernel(place, mine, other, w_mine, w_other, kept, sent, total):
    step = pl.program_id(0)
    depth = pl.num_programs(0)
    contract = (((1,), (1,)), ((), ()))
    rows = total.shape[1]
    part = lax.dot_general(
        w_mine[...], mine[...].reshape(rows, -1), contract, preferred_element_type=f32
    ) + lax.dot_general(
        w_other[...], other[...].reshape(rows, -1), contract, preferred_element_type=f32
    )

    @pl.when(step == 0)
    def _():
        total[...] = part

    @pl.when(step > 0)
    def _():
        total[...] += part

    half = rows // 2

    @pl.when((step == depth - 1) & (place[0] == 0))
    def _():
        kept[...] = total[:, :half]
        sent[...] = total[:, half:]

    @pl.when((step == depth - 1) & (place[0] == 1))
    def _():
        kept[...] = total[:, half:]
        sent[...] = total[:, :half]


def logits_of(place, mine, other, weights):
    blocks, depth, rows, width = mine.shape
    columns = weights.shape[0]
    row_total = blocks * rows
    hidden_spec = pl.BlockSpec((blocks, 1, rows, width), lambda z, s: (0, z, 0, 0))
    out = jax.ShapeDtypeStruct((columns, row_total // 2), f32)
    out_spec = pl.BlockSpec(out.shape, lambda z, s: (0, 0))
    return pl.pallas_call(
        logits_kernel,
        grid_spec=pltpu.PrefetchScalarGridSpec(
            num_scalar_prefetch=1,
            grid=(depth,),
            in_specs=[
                hidden_spec,
                hidden_spec,
                pl.BlockSpec((columns, width), lambda z, s: (0, 2 * z + s[1])),
                pl.BlockSpec((columns, width), lambda z, s: (0, 2 * z + 1 - s[1])),
            ],
            out_specs=[out_spec, out_spec],
            scratch_shapes=[pltpu.VMEM((columns, row_total), f32)],
        ),
        out_shape=[out, out],
        compiler_params=PARAMS,
        name="logits",
    )(place, mine, other, weights, weights)


def stats_kernel(place, kept, got, out):
    def write(policy, refer):
        mixed = (1.0 - BETA) * policy + BETA * refer
        top = jnp.max(policy, 0, keepdims=True)
        mixed_top = jnp.max(mixed, 0, keepdims=True)
        weight = jnp.exp(policy - top)
        total = jnp.sum(weight, 0, keepdims=True)
        cross = jnp.sum(weight * (policy - mixed), 0, keepdims=True) / total
        mixed_total = jnp.sum(jnp.exp(mixed - mixed_top), 0, keepdims=True)
        lines = (top + jnp.log(total), cross, mixed_top + jnp.log(mixed_total))
        out[...] = spread(lines, out.shape)

    @pl.when(place[0] == 0)
    def _():
        write(kept[...], got[...])

    @pl.when(place[0] == 1)
    def _():
        write(got[...], kept[...])


def spread(lines, shape):
    count, height, width = shape
    tail = jnp.zeros((height - len(lines), width), f32)
    tile = jnp.concatenate([*lines, tail], 0)
    return jnp.broadcast_to(tile[None], shape)


def merged(tiles):
    top = jnp.max(tiles, 0)
    weight = jnp.exp(tiles - top[None])
    total = jnp.sum(weight, 0)
    lse = top + jnp.log(total)
    cross = jnp.sum(weight[:, 0:1] * tiles[:, 1:2], 0) / total[0:1]
    return lse[0:1], cross, lse[2:3]


def merge_kernel(tiles, out):
    out[...] = spread(merged(tiles[...]), out.shape)


def final_kernel(tiles, out):
    count = tiles.shape[0] // 2
    half = tiles.shape[2]
    for k in range(2):
        policy_lse, cross, mixture_lse = merged(tiles[k * count : (k + 1) * count])
        divergence = cross - policy_lse + mixture_lse
        lines = (policy_lse, divergence, mixture_lse)
        out[:, k * half : (k + 1) * half] = spread(lines, (1, 8, half))[0]


def grads_kernel(
    place, kept, got, sent, late, final, ids, kl_weight, advantage, w_mine, w_other,
    kept_out, sent_out, flat, turned,
):
    columns, half = kept.shape
    padded = flat.shape[0]

    def fill(low, high, policy_head):
        for k, (own_ref, partner_ref) in enumerate((low, high)):
            at = slice(k * half, (k + 1) * half)
            policy_lse, divergence, mixture_lse = (final[i : i + 1, at] for i in range(3))
            kl = kl_weight[:, at]
            adv = advantage[:, at]
            token = ids[:, at] - place[2]

            def rows(i, _, own_ref=own_ref, partner_ref=partner_ref):
                start = pl.multiple_of(i * STEP, STEP)
                own, partner = own_ref[pl.ds(start, STEP)], partner_ref[pl.ds(start, STEP)]
                policy, refer = (own, partner) if policy_head else (partner, own)
                mixed = (1.0 - BETA) * policy + BETA * refer
                policy_prob = jnp.exp(policy - policy_lse)
                mixture_prob = jnp.exp(mixed - mixture_lse)
                shift = mixture_prob - policy_prob
                if policy_head:
                    gap = policy - policy_lse - mixed + mixture_lse
                    column = start + lax.broadcasted_iota(jnp.int32, (STEP, half), 0)
                    chosen = (token == column).astype(f32)
                    grad = kl * (
                        policy_prob * (gap - divergence) + (1.0 - BETA) * shift
                    ) - adv * (chosen - policy_prob)
                else:
                    grad = BETA * kl * shift
                flat[pl.ds(start, STEP), at] = grad
                return _

            lax.fori_loop(0, columns // STEP, rows, None, unroll=True)
        flat[columns:, :] = jnp.zeros((padded - columns, flat.shape[1]), f32)
        for start in range(0, padded, LANES):
            turned[:, start : start + LANES] = flat[start : start + LANES, :].T.astype(bf16)

    @pl.when((pl.program_id(0) == 0) & (place[0] == 0))
    def _():
        fill((kept, got), (sent, late), True)

    @pl.when((pl.program_id(0) == 0) & (place[0] == 1))
    def _():
        fill((sent, late), (kept, got), False)

    grad = turned[:, :columns]
    contract = (((1,), (0,)), ((), ()))
    mine = lax.dot_general(grad, w_mine[...], contract, preferred_element_type=f32)
    kept_out[...] = mine.reshape(kept_out.shape)
    other = lax.dot_general(grad, w_other[...], contract, preferred_element_type=f32)
    sent_out[...] = other.astype(bf16).reshape(sent_out.shape)


def grads_of(place, kept, got, sent, late, final, ids, kl_weight, advantage, weights, shape):
    blocks, depth, rows, width = shape
    columns = weights.shape[0]
    row_total = blocks * rows
    whole = lambda a: pl.BlockSpec(a.shape, lambda z, s: (0, 0))
    spec = pl.BlockSpec((blocks, 1, rows, width), lambda z, s: (0, z, 0, 0))
    small = [kept, got, sent, late, final, ids, kl_weight, advantage]
    padded = -(-columns // LANES) * LANES
    return pl.pallas_call(
        grads_kernel,
        grid_spec=pltpu.PrefetchScalarGridSpec(
            num_scalar_prefetch=1,
            grid=(depth,),
            in_specs=[
                *(whole(a) for a in small),
                pl.BlockSpec((columns, width), lambda z, s: (0, 2 * z + s[1])),
                pl.BlockSpec((columns, width), lambda z, s: (0, 2 * z + 1 - s[1])),
            ],
            out_specs=[spec, spec],
            scratch_shapes=[
                pltpu.VMEM((padded, row_total), f32),
                pltpu.VMEM((row_total, padded), bf16),
            ],
        ),
        out_shape=[jax.ShapeDtypeStruct(shape, f32), jax.ShapeDtypeStruct(shape, bf16)],
        compiler_params=PARAMS,
        name="grads",
    )(place, *small, weights, weights)


def on_core(kernel, shape, specs, name):
    return pl.pallas_call(
        kernel,
        in_specs=specs,
        out_specs=VMEM,
        out_shape=jax.ShapeDtypeStruct(shape, f32),
        compiler_params=PARAMS,
        name=name,
    )


def body(hidden, head_weights, token_ids, kl_weight, advantage):
    rows, width = hidden.shape
    columns = head_weights.shape[1]
    row_blocks = lax.axis_size((XLO, Y))
    depth = lax.axis_size(Z)
    chips = row_blocks * depth
    row_total = rows * row_blocks
    half = row_total // 2
    col_start = lax.axis_index((XLO, Y, Z, CORE)) * columns
    place = jnp.stack([lax.axis_index(HEAD), lax.axis_index(CORE), col_start]).astype(jnp.int32)
    weights = head_weights.T

    mine = lax.all_to_all(
        jnp.broadcast_to(hidden[None], (chips, rows, width)), CHIPS, 0, 0, tiled=True
    )
    other = lax.ppermute(mine, CORE, SWAP)
    shape = (row_blocks, depth, rows, width)
    kept, sent = logits_of(place, mine.reshape(shape), other.reshape(shape), weights)

    got = lax.ppermute(sent, HEAD, SWAP)
    narrow, wide = lax.axis_size(NARROW), lax.axis_size(WIDE)
    stats = on_core(stats_kernel, (narrow, 8, half), [SMEM, VMEM, VMEM], "stats")(place, kept, got)
    kept_late, stats = lax.optimization_barrier((kept, stats))
    late = lax.ppermute(kept_late, HEAD, SWAP)
    stats = lax.all_to_all(stats, NARROW, 0, 0, tiled=True)
    stats = on_core(merge_kernel, (wide, 8, half), [VMEM], "merge")(stats)
    stats = lax.all_to_all(stats, WIDE, 0, 0, tiled=True)
    final = on_core(final_kernel, (8, row_total), [VMEM], "final")(stats)

    line = lambda a: a.reshape(1, row_total)
    kept_part, sent_part = grads_of(
        place, kept, got, sent, late, final, line(token_ids), line(kl_weight), line(advantage),
        weights, shape,
    )
    back = lax.ppermute(sent_part, CORE, SWAP)
    pair_sum = (kept_part + back.astype(f32)).astype(bf16).reshape(chips, rows, width)
    arrived = lax.all_to_all(pair_sum, CHIPS, 0, 0, tiled=True)
    hidden_grad = jnp.sum(arrived.astype(f32), 0).T
    return (hidden_grad, final[2], final[1])


def solution(mesh):
    finer = Mesh(mesh.devices.reshape(2, 2, 8, 8, 2), (HEAD, XLO, Y, Z, CORE))
    return jax.shard_map(
        body,
        mesh=finer,
        in_specs=(P(WIDE, NARROW), P(None, (*WIDE, *NARROW)), P(), P(), P()),
        out_specs=(P(NARROW, WIDE), P(), P()),
        check_vma=False,
    )
```

```python
import jax
import jax.numpy as jnp
from jax import lax
from jax.experimental import pallas as pl
from jax.experimental.pallas import tpu as pltpu
from jax.sharding import Mesh
from jax.sharding import PartitionSpec as P

HEAD, XLO, YHI, YLO, ZHI, ZLO, CORE = "head", "xlo", "yhi", "ylo", "zhi", "zlo", "core"
Y = (YHI, YLO)
Z = (ZHI, ZLO)
NARROW = (*Z, CORE)
WIDE = (HEAD, XLO, *Y)
GATHER_FAR, GATHER_NEAR = (*Y, ZHI), (XLO, ZLO)
REDUCE_NEAR, REDUCE_FAR = (YLO, ZLO), (XLO, YHI, ZHI)

BETA = 0.2
SWAP = [(0, 1), (1, 0)]
LANES = 128
STEP = 16
f32 = jnp.float32
bf16 = jnp.bfloat16
VMEM = pl.BlockSpec(memory_space=pltpu.VMEM)
HBM = pl.BlockSpec(memory_space=pltpu.HBM)
SMEM = pl.BlockSpec(memory_space=pltpu.SMEM)
WIDE_PARAMS = pltpu.CompilerParams(vmem_limit_bytes=50 << 20)
PARAMS = pltpu.CompilerParams(vmem_limit_bytes=16 << 20)


def fetches(weights, core, buffer, sems):
    depth, _, width = buffer.shape
    copies = []
    for z in range(depth):
        start = pl.multiple_of((2 * z + core) * width, width)
        copies.append(
            pltpu.make_async_copy(weights.at[:, pl.ds(start, width)], buffer.at[z], sems.at[z])
        )
        copies[z].start()
    return copies


def products(blocks, copies, buffer):
    xlo, zlo, y, zhi, rows, width = blocks.shape
    total = None
    for z, copy in enumerate(copies):
        hi, lo = z // zlo, z % zlo
        copy.wait()
        part = lax.dot_general(
            buffer[z],
            blocks[:, lo, :, hi].reshape(xlo * y * rows, width),
            (((1,), (1,)), ((), ())),
            preferred_element_type=f32,
        )
        total = part if total is None else total + part
    return total


def first_kernel(place, mine, weights, out, buffer, sems):
    out[...] = products(mine, fetches(weights, place[1], buffer, sems), buffer)


def second_kernel(place, part, other, weights, kept, sent, buffer, sems):
    copies = fetches(weights, 1 - place[1], buffer, sems)
    total = part[...] + products(other, copies, buffer)
    half = kept.shape[1]

    @pl.when(place[0] == 0)
    def _():
        kept[...] = total[:, :half]
        sent[...] = total[:, half:]

    @pl.when(place[0] == 1)
    def _():
        kept[...] = total[:, half:]
        sent[...] = total[:, :half]


def stats_kernel(place, kept, got, out):
    def write(policy, refer):
        mixed = (1.0 - BETA) * policy + BETA * refer
        top = jnp.max(policy, 0, keepdims=True)
        mixed_top = jnp.max(mixed, 0, keepdims=True)
        weight = jnp.exp(policy - top)
        total = jnp.sum(weight, 0, keepdims=True)
        cross = jnp.sum(weight * (policy - mixed), 0, keepdims=True) / total
        mixed_total = jnp.sum(jnp.exp(mixed - mixed_top), 0, keepdims=True)
        lines = (top + jnp.log(total), cross, mixed_top + jnp.log(mixed_total))
        out[...] = spread(lines, out.shape)

    @pl.when(place[0] == 0)
    def _():
        write(kept[...], got[...])

    @pl.when(place[0] == 1)
    def _():
        write(got[...], kept[...])


def spread(lines, shape):
    count, height, width = shape
    tail = jnp.zeros((height - len(lines), width), f32)
    tile = jnp.concatenate([*lines, tail], 0)
    return jnp.broadcast_to(tile[None], shape)


def merged(tiles):
    top = jnp.max(tiles, 0)
    weight = jnp.exp(tiles - top[None])
    total = jnp.sum(weight, 0)
    lse = top + jnp.log(total)
    cross = jnp.sum(weight[:, 0:1] * tiles[:, 1:2], 0) / total[0:1]
    return lse[0:1], cross, lse[2:3]


def merge_kernel(tiles, out):
    out[...] = spread(merged(tiles[...]), out.shape)


def final_kernel(tiles, out):
    count = tiles.shape[0] // 2
    half = tiles.shape[2]
    for k in range(2):
        policy_lse, cross, mixture_lse = merged(tiles[k * count : (k + 1) * count])
        divergence = cross - policy_lse + mixture_lse
        lines = (policy_lse, divergence, mixture_lse)
        out[:, k * half : (k + 1) * half] = spread(lines, (1, 8, half))[0]


def sent_kernel(
    place, kept, got, sent, late, final, ids, kl_weight, advantage, weights,
    turned, sent_out, flat, buffer, sems,
):
    copies = fetches(weights, 1 - place[1], buffer, sems)
    columns, half = kept.shape
    padded = flat.shape[0]

    def fill(low, high, policy_head):
        for k, (own_ref, partner_ref) in enumerate((low, high)):
            at = slice(k * half, (k + 1) * half)
            policy_lse, divergence, mixture_lse = (final[i : i + 1, at] for i in range(3))
            kl = kl_weight[:, at]
            adv = advantage[:, at]
            token = ids[:, at] - place[2]

            def rows(i, _, own_ref=own_ref, partner_ref=partner_ref):
                start = pl.multiple_of(i * STEP, STEP)
                own, partner = own_ref[pl.ds(start, STEP)], partner_ref[pl.ds(start, STEP)]
                policy, refer = (own, partner) if policy_head else (partner, own)
                mixed = (1.0 - BETA) * policy + BETA * refer
                policy_prob = jnp.exp(policy - policy_lse)
                mixture_prob = jnp.exp(mixed - mixture_lse)
                shift = mixture_prob - policy_prob
                if policy_head:
                    gap = policy - policy_lse - mixed + mixture_lse
                    column = start + lax.broadcasted_iota(jnp.int32, (STEP, half), 0)
                    chosen = (token == column).astype(f32)
                    grad = kl * (
                        policy_prob * (gap - divergence) + (1.0 - BETA) * shift
                    ) - adv * (chosen - policy_prob)
                else:
                    grad = BETA * kl * shift
                flat[pl.ds(start, STEP), at] = grad
                return _

            lax.fori_loop(0, columns // STEP, rows, None, unroll=True)
        flat[columns:, :] = jnp.zeros((padded - columns, flat.shape[1]), f32)
        for start in range(0, padded, LANES):
            turned[:, start : start + LANES] = flat[start : start + LANES, :].T.astype(bf16)

    @pl.when(place[0] == 0)
    def _():
        fill((kept, got), (sent, late), True)

    @pl.when(place[0] == 1)
    def _():
        fill((sent, late), (kept, got), False)

    for z, part in sums(turned, copies, buffer):
        sent_out[z] = part.astype(bf16)


def sums(turned, copies, buffer):
    grad = turned[:, : buffer.shape[1]]
    for z, copy in enumerate(copies):
        copy.wait()
        yield z, lax.dot_general(
            grad, buffer[z], (((1,), (0,)), ((), ())), preferred_element_type=f32
        )


def pair_kernel(place, turned, back, weights, out, buffer, sems):
    ylo, zlo, xlo, yhi, zhi, rows, width = out.shape
    copies = fetches(weights, place[1], buffer, sems)
    for z, part in sums(turned, copies, buffer):
        whole = (part + back[z].astype(f32)).astype(bf16)
        whole = whole.reshape(xlo, yhi, ylo, rows, width)
        for lo in range(ylo):
            out[lo, z % zlo, :, :, z // zlo] = whole[:, :, lo]


def on_core(kernel, out_shape, count, name, scalars=True, scratch=(), hbm=0):
    return pl.pallas_call(
        kernel,
        in_specs=[SMEM] * scalars + [VMEM] * count + [HBM] * hbm,
        out_specs=jax.tree.map(lambda _: VMEM, out_shape),
        out_shape=out_shape,
        scratch_shapes=scratch,
        compiler_params=WIDE_PARAMS if hbm else PARAMS,
        name=name,
    )


def array(shape, dtype=f32):
    return jax.ShapeDtypeStruct(shape, dtype)


def copies(block, axes):
    count = lax.axis_size(axes)
    return lax.all_to_all(
        jnp.broadcast_to(block[None], (count, *block.shape)), axes, 0, 0, tiled=True
    )


def exchange_sum(parts, axes):
    return jnp.sum(lax.all_to_all(parts, axes, 0, 0, tiled=True).astype(f32), 0)


def body(hidden, head_weights, token_ids, kl_weight, advantage):
    rows, width = hidden.shape
    columns = head_weights.shape[1]
    xlo, yhi, ylo, zhi, zlo = (lax.axis_size(a) for a in (XLO, YHI, YLO, ZHI, ZLO))
    depth = zhi * zlo
    row_total = rows * xlo * yhi * ylo
    half = row_total // 2
    col_start = lax.axis_index((XLO, *Y, *Z, CORE)) * columns
    place = jnp.stack([lax.axis_index(HEAD), lax.axis_index(CORE), col_start]).astype(jnp.int32)
    weights = head_weights.T
    fetch = [pltpu.VMEM((depth, columns, width), bf16), pltpu.SemaphoreType.DMA((depth,))]

    mine = copies(copies(hidden, GATHER_FAR), GATHER_NEAR)
    other = lax.ppermute(mine, CORE, SWAP)
    shape = (xlo, zlo, yhi * ylo, zhi, rows, width)
    part = on_core(first_kernel, array((columns, row_total)), 1, "first", scratch=fetch, hbm=1)(
        place, mine.reshape(shape), weights
    )
    kept, sent = on_core(
        second_kernel, [array((columns, half))] * 2, 2, "second", scratch=fetch, hbm=1
    )(place, part, other.reshape(shape), weights)

    got = lax.ppermute(sent, HEAD, SWAP)
    narrow, wide = lax.axis_size(NARROW), lax.axis_size(WIDE)
    stats = on_core(stats_kernel, array((narrow, 8, half)), 2, "stats")(place, kept, got)
    kept_late, stats = lax.optimization_barrier((kept, stats))
    late = lax.ppermute(kept_late, HEAD, SWAP)
    stats = lax.all_to_all(stats, NARROW, 0, 0, tiled=True)
    stats = on_core(merge_kernel, array((wide, 8, half)), 1, "merge", False)(stats)
    stats = lax.all_to_all(stats, WIDE, 0, 0, tiled=True)
    final = on_core(final_kernel, array((8, row_total)), 1, "final", False)(stats)

    line = lambda a: a.reshape(1, row_total)
    padded = -(-columns // LANES) * LANES
    turned, sent_part = on_core(
        sent_kernel,
        [array((row_total, padded), bf16), array((depth, row_total, width), bf16)],
        8,
        "sent_part",
        scratch=[pltpu.VMEM((padded, row_total), f32), *fetch],
        hbm=1,
    )(
        place, kept, got, sent, late, final, line(token_ids), line(kl_weight), line(advantage),
        weights,
    )
    back = lax.ppermute(sent_part, CORE, SWAP)
    pair_sum = on_core(
        pair_kernel,
        array((ylo, zlo, xlo, yhi, zhi, rows, width), bf16),
        2,
        "pair_sum",
        scratch=fetch,
        hbm=1,
    )(place, turned, back, weights)
    near = exchange_sum(pair_sum.reshape(ylo * zlo, -1, width), REDUCE_NEAR).astype(bf16)
    hidden_grad = exchange_sum(near.reshape(-1, rows, width), REDUCE_FAR).T
    return (hidden_grad, final[2], final[1])


def solution(mesh):
    finer = Mesh(mesh.devices.reshape(2, 2, 4, 2, 4, 2, 2), (*WIDE, *NARROW))
    return jax.shard_map(
        body,
        mesh=finer,
        in_specs=(P(WIDE, NARROW), P(None, (*WIDE, *NARROW)), P(), P(), P()),
        out_specs=(P(NARROW, WIDE), P(), P()),
        check_vma=False,
    )
```

```python
import jax
import jax.numpy as jnp
from jax import lax
from jax.experimental import pallas as pl
from jax.experimental.pallas import tpu as pltpu
from jax.sharding import Mesh
from jax.sharding import PartitionSpec as P

HEAD, XLO, YHI, YLO, ZHI, ZLO, CORE = "head", "xlo", "yhi", "ylo", "zhi", "zlo", "core"
Y = (YHI, YLO)
Z = (ZHI, ZLO)
NARROW = (*Z, CORE)
WIDE = (HEAD, XLO, *Y)
GATHER_FAR, GATHER_NEAR = (*Y, ZHI), (XLO, ZLO)
STATS_NEAR, STATS_FAR = (HEAD, XLO, YLO, ZLO, CORE), (YHI, ZHI)
REDUCE_NEAR, REDUCE_FAR = (XLO, YLO, ZLO), (YHI, ZHI)

BETA = 0.2
SWAP = [(0, 1), (1, 0)]
LANES = 128
STEP = 16
f32 = jnp.float32
bf16 = jnp.bfloat16
ANY = pl.BlockSpec(memory_space=pl.ANY)
VMEM = pl.BlockSpec(memory_space=pltpu.VMEM)
SMEM = pl.BlockSpec(memory_space=pltpu.SMEM)
WIDE_PARAMS = pltpu.CompilerParams(vmem_limit_bytes=48 << 20)
WIDER_PARAMS = pltpu.CompilerParams(vmem_limit_bytes=50 << 20)
PARAMS = pltpu.CompilerParams(vmem_limit_bytes=16 << 20)


def hold_kernel(place, weights, mine, other, sems):
    depth = sems.shape[1]
    width = mine.shape[1] // depth
    copies = []
    for side, out in enumerate((mine, other)):
        core = place[1] if side == 0 else 1 - place[1]
        for z in range(depth):
            start = pl.multiple_of((2 * z + core) * width, width)
            source = weights.at[:, pl.ds(start, width)]
            target = out.at[:, z * width : (z + 1) * width]
            copies.append(pltpu.make_async_copy(source, target, sems.at[side, z]))
            copies[-1].start()
    for copy in copies:
        copy.wait()


def held(place, weights, depth):
    columns, features = weights.shape
    half = pltpu.HBM((columns, features // 2), weights.dtype)
    return pl.pallas_call(
        hold_kernel,
        in_specs=[SMEM, ANY],
        out_specs=[ANY, ANY],
        out_shape=[half, half],
        scratch_shapes=[pltpu.SemaphoreType.DMA((2, depth))],
        compiler_params=PARAMS,
        name="hold",
    )(place, weights)


def fetch(sources, targets, sems):
    copies = [
        pltpu.make_async_copy(source, target, sems.at[k])
        for k, (source, target) in enumerate(zip(sources, targets))
    ]
    for copy in copies:
        copy.start()
    return copies


def flatten(blocks, flat):
    xlo, zlo, y, zhi, rows, width = blocks.shape
    for z in range(zhi * zlo):
        part = blocks[:, z % zlo, :, z // zlo].reshape(xlo * y * rows, width)
        flat[:, z * width : (z + 1) * width] = part


def product(weights, flat):
    return lax.dot_general(
        weights[...], flat[...], (((1,), (1,)), ((), ())), preferred_element_type=f32
    )


def first_kernel(mine, w_mine, w_other, out, next_weights, flat, here, sems):
    copies = fetch((w_mine, w_other), (here, next_weights), sems)
    flatten(mine, flat)
    copies[0].wait()
    out[...] = product(here, flat)
    copies[1].wait()


def second_kernel(place, part, other, weights, kept, sent, flat):
    flatten(other, flat)
    total = part[...] + product(weights, flat)
    half = kept.shape[1]

    @pl.when(place[0] == 0)
    def _():
        kept[...] = total[:, :half]
        sent[...] = total[:, half:]

    @pl.when(place[0] == 1)
    def _():
        kept[...] = total[:, half:]
        sent[...] = total[:, :half]


def stats_kernel(place, kept, got, out):
    def write(policy, refer):
        mixed = (1.0 - BETA) * policy + BETA * refer
        top = jnp.max(policy, 0, keepdims=True)
        mixed_top = jnp.max(mixed, 0, keepdims=True)
        weight = jnp.exp(policy - top)
        total = jnp.sum(weight, 0, keepdims=True)
        cross = jnp.sum(weight * (policy - mixed), 0, keepdims=True) / total
        mixed_total = jnp.sum(jnp.exp(mixed - mixed_top), 0, keepdims=True)
        lines = (top + jnp.log(total), cross, mixed_top + jnp.log(mixed_total))
        out[...] = spread(lines, out.shape)

    @pl.when(place[0] == 0)
    def _():
        write(kept[...], got[...])

    @pl.when(place[0] == 1)
    def _():
        write(got[...], kept[...])


def spread(lines, shape):
    count, height, width = shape
    tail = jnp.zeros((height - len(lines), width), f32)
    tile = jnp.concatenate([*lines, tail], 0)
    return jnp.broadcast_to(tile[None], shape)


def merged(tiles):
    top = jnp.max(tiles, 0)
    weight = jnp.exp(tiles - top[None])
    total = jnp.sum(weight, 0)
    lse = top + jnp.log(total)
    cross = jnp.sum(weight[:, 0:1] * tiles[:, 1:2], 0) / total[0:1]
    return lse[0:1], cross, lse[2:3]


def both_heads(tiles):
    sides = [merged(tiles[k]) for k in range(2)]
    return [jnp.concatenate(pair, 1) for pair in zip(*sides)]


def merge_kernel(tiles, out):
    out[...] = spread(both_heads(tiles), out.shape)


def final_kernel(tiles, out):
    policy_lse, cross, mixture_lse = merged(tiles[...])
    lines = (policy_lse, cross - policy_lse + mixture_lse, mixture_lse)
    out[...] = spread(lines, (1, *out.shape))[0]


def sent_kernel(
    place, kept, got, sent, late, final, ids, kl_weight, advantage, w_other,
    turned, sent_out, flat, here, sems,
):
    copies = fetch((w_other,), (here,), sems)
    columns, half = kept.shape
    padded = flat.shape[0]

    def fill(low, high, policy_head):
        for k, (own_ref, partner_ref) in enumerate((low, high)):
            at = slice(k * half, (k + 1) * half)
            policy_lse, divergence, mixture_lse = (final[i : i + 1, at] for i in range(3))
            kl = kl_weight[:, at]
            adv = advantage[:, at]
            token = ids[:, at] - place[2]

            def rows(i, _, own_ref=own_ref, partner_ref=partner_ref):
                start = pl.multiple_of(i * STEP, STEP)
                own, partner = own_ref[pl.ds(start, STEP)], partner_ref[pl.ds(start, STEP)]
                policy, refer = (own, partner) if policy_head else (partner, own)
                mixed = (1.0 - BETA) * policy + BETA * refer
                policy_prob = jnp.exp(policy - policy_lse)
                mixture_prob = jnp.exp(mixed - mixture_lse)
                shift = mixture_prob - policy_prob
                if policy_head:
                    gap = policy - policy_lse - mixed + mixture_lse
                    column = start + lax.broadcasted_iota(jnp.int32, (STEP, half), 0)
                    chosen = (token == column).astype(f32)
                    grad = kl * (
                        policy_prob * (gap - divergence) + (1.0 - BETA) * shift
                    ) - adv * (chosen - policy_prob)
                else:
                    grad = BETA * kl * shift
                flat[pl.ds(start, STEP), at] = grad
                return _

            lax.fori_loop(0, columns // STEP, rows, None, unroll=True)
        flat[columns:, :] = jnp.zeros((padded - columns, flat.shape[1]), f32)
        for start in range(0, padded, LANES):
            turned[:, start : start + LANES] = flat[start : start + LANES, :].T.astype(bf16)

    @pl.when(place[0] == 0)
    def _():
        fill((kept, got), (sent, late), True)

    @pl.when(place[0] == 1)
    def _():
        fill((sent, late), (kept, got), False)

    copies[0].wait()
    for at, part in sums(turned, here):
        sent_out[:, at] = part.astype(bf16)


def sums(turned, weights, step=512):
    columns, features = weights.shape
    grad = turned[:, :columns]
    for start in range(0, features, step):
        at = slice(start, start + step)
        yield at, lax.dot_general(
            grad, weights[:, at], (((1,), (0,)), ((), ())), preferred_element_type=f32
        )


def own_kernel(turned, w_mine, out, here, sems):
    copies = fetch((w_mine,), (here,), sems)
    copies[0].wait()
    for at, part in sums(turned, here):
        out[:, at] = part


def pair_kernel(partial, back, out):
    xlo, ylo, zlo, yhi, zhi, rows, width = out.shape
    for z in range(zhi * zlo):
        at = slice(z * width, (z + 1) * width)
        whole = (partial[:, at] + back[:, at].astype(f32)).astype(bf16)
        whole = whole.reshape(xlo, yhi, ylo, rows, width)
        for lo in range(ylo):
            out[:, lo, z % zlo, :, z // zlo] = whole[:, :, lo]


def on_core(kernel, out_shape, count, name, scalars=True, scratch=(), hbm=0):
    return pl.pallas_call(
        kernel,
        in_specs=[SMEM] * scalars + [VMEM] * count + [ANY] * hbm,
        out_specs=jax.tree.map(lambda _: VMEM, out_shape),
        out_shape=out_shape,
        scratch_shapes=scratch,
        compiler_params=(PARAMS, WIDER_PARAMS, WIDE_PARAMS)[hbm],
        name=name,
    )


def array(shape, dtype=f32):
    return jax.ShapeDtypeStruct(shape, dtype)


def copies(block, axes):
    count = lax.axis_size(axes)
    return lax.all_to_all(
        jnp.broadcast_to(block[None], (count, *block.shape)), axes, 0, 0, tiled=True
    )


def exchange_sum(parts, axes):
    return jnp.sum(lax.all_to_all(parts, axes, 0, 0, tiled=True).astype(f32), 0)


def body(hidden, head_weights, token_ids, kl_weight, advantage):
    rows, width = hidden.shape
    columns = head_weights.shape[1]
    xlo, yhi, ylo, zhi, zlo = (lax.axis_size(a) for a in (XLO, YHI, YLO, ZHI, ZLO))
    depth = zhi * zlo
    row_total = rows * xlo * yhi * ylo
    half = row_total // 2
    col_start = lax.axis_index((XLO, *Y, *Z, CORE)) * columns
    place = jnp.stack([lax.axis_index(HEAD), lax.axis_index(CORE), col_start]).astype(jnp.int32)
    w_mine, w_other = held(place, head_weights.T, depth)
    flat = [pltpu.VMEM((row_total, depth * width), bf16)]

    far = copies(hidden, GATHER_FAR)
    far, w_mine, w_other = lax.optimization_barrier((far, w_mine, w_other))
    mine = copies(far, GATHER_NEAR)
    other = lax.ppermute(mine, CORE, SWAP)
    shape = (xlo, zlo, yhi * ylo, zhi, rows, width)
    w_half = array((columns, depth * width), bf16)
    buffers = [pltpu.VMEM(w_half.shape, bf16), pltpu.SemaphoreType.DMA((2,))]
    part, w_next = on_core(
        first_kernel,
        [array((columns, row_total)), w_half],
        1,
        "first",
        False,
        scratch=flat + buffers,
        hbm=2,
    )(mine.reshape(shape), w_mine, w_other)
    kept, sent = on_core(
        second_kernel, [array((columns, half))] * 2, 3, "second", scratch=flat
    )(place, part, other.reshape(shape), w_next)

    got = lax.ppermute(sent, HEAD, SWAP)
    near, far = lax.axis_size(STATS_NEAR), lax.axis_size(STATS_FAR)
    stats = on_core(stats_kernel, array((near, 8, half)), 2, "stats")(place, kept, got)
    kept_late, stats = lax.optimization_barrier((kept, stats))
    late = lax.ppermute(kept_late, HEAD, SWAP)
    stats = lax.all_to_all(stats, STATS_NEAR, 0, 0, tiled=True).reshape(2, near // 2, 8, half)
    stats = on_core(merge_kernel, array((far, 8, row_total)), 1, "merge", False)(stats)
    stats = lax.all_to_all(stats, STATS_FAR, 0, 0, tiled=True)
    final = on_core(final_kernel, array((8, row_total)), 1, "final", False)(stats)

    line = lambda a: a.reshape(1, row_total)
    padded = -(-columns // LANES) * LANES
    wide_rows = (row_total, depth * width)
    turned, sent_part = on_core(
        sent_kernel,
        [array((row_total, padded), bf16), array(wide_rows, bf16)],
        8,
        "sent_part",
        scratch=[pltpu.VMEM((padded, row_total), f32), *buffers],
        hbm=1,
    )(
        place, kept, got, sent, late, final, line(token_ids), line(kl_weight), line(advantage),
        w_other,
    )
    back = lax.ppermute(sent_part, CORE, SWAP)
    partial = on_core(own_kernel, array(wide_rows), 1, "own", False, scratch=buffers, hbm=1)(
        turned, w_mine
    )
    pair_sum = on_core(
        pair_kernel, array((xlo, ylo, zlo, yhi, zhi, rows, width), bf16), 2, "pair_sum", False
    )(partial, back)
    near = exchange_sum(pair_sum.reshape(xlo * ylo * zlo, -1, width), REDUCE_NEAR).astype(bf16)
    hidden_grad = exchange_sum(near.reshape(-1, rows, width), REDUCE_FAR).T
    return (hidden_grad, final[2], final[1])


def solution(mesh):
    finer = Mesh(mesh.devices.reshape(2, 2, 4, 2, 4, 2, 2), (*WIDE, *NARROW))
    return jax.shard_map(
        body,
        mesh=finer,
        in_specs=(P(WIDE, NARROW), P(None, (*WIDE, *NARROW)), P(), P(), P()),
        out_specs=(P(NARROW, WIDE), P(), P()),
        check_vma=False,
    )
```

```python
import jax
import jax.numpy as jnp
from jax import lax
from jax.experimental import pallas as pl
from jax.experimental.pallas import tpu as pltpu
from jax.sharding import Mesh
from jax.sharding import PartitionSpec as P

HEAD, XLO, YHI, YLO, ZHI, ZLO, CORE = "head", "xlo", "yhi", "ylo", "zhi", "zlo", "core"
Y = (YHI, YLO)
Z = (ZHI, ZLO)
NARROW = (*Z, CORE)
WIDE = (HEAD, XLO, *Y)
FAR = (XLO, YHI, ZHI)
STATS_NEAR, STATS_FAR = NARROW, WIDE

BETA = 0.2
SWAP = [(0, 1), (1, 0)]
LANES = 128
STEP = 16
f32 = jnp.float32
bf16 = jnp.bfloat16
ANY = pl.BlockSpec(memory_space=pl.ANY)
VMEM = pl.BlockSpec(memory_space=pltpu.VMEM)
SMEM = pl.BlockSpec(memory_space=pltpu.SMEM)
WIDE_PARAMS = pltpu.CompilerParams(vmem_limit_bytes=48 << 20)
WIDER_PARAMS = pltpu.CompilerParams(vmem_limit_bytes=50 << 20)
PARAMS = pltpu.CompilerParams(vmem_limit_bytes=16 << 20)


def hold_kernel(place, weights, mine, other, sems):
    depth = sems.shape[1]
    width = mine.shape[1] // depth
    copies = []
    for side, out in enumerate((mine, other)):
        core = place[1] if side == 0 else 1 - place[1]
        for z in range(depth):
            start = pl.multiple_of((2 * z + core) * width, width)
            source = weights.at[:, pl.ds(start, width)]
            target = out.at[:, z * width : (z + 1) * width]
            copies.append(pltpu.make_async_copy(source, target, sems.at[side, z]))
            copies[-1].start()
    for copy in copies:
        copy.wait()


def held(place, weights, depth):
    columns, features = weights.shape
    half = pltpu.HBM((columns, features // 2), weights.dtype)
    return pl.pallas_call(
        hold_kernel,
        in_specs=[SMEM, ANY],
        out_specs=[ANY, ANY],
        out_shape=[half, half],
        scratch_shapes=[pltpu.SemaphoreType.DMA((2, depth))],
        compiler_params=PARAMS,
        name="hold",
    )(place, weights)


def fetch(sources, targets, sems, pieces=4):
    copies = []
    for k, (source, target) in enumerate(zip(sources, targets)):
        tiles = source.shape[0] // STEP
        for piece in range(pieces):
            low, high = (STEP * (tiles * i // pieces) for i in (piece, piece + 1))
            copies.append(
                pltpu.make_async_copy(
                    source.at[low:high], target.at[low:high], sems.at[k * pieces + piece]
                )
            )
    for copy in copies:
        copy.start()
    return copies


def flatten(blocks, flat):
    ylo, zlo, xlo, yhi, zhi, rows, width = blocks.shape
    for k in range(xlo * yhi * ylo):
        x, y_hi, y_lo = k // (yhi * ylo), k // ylo % yhi, k % ylo
        for z in range(zhi * zlo):
            flat[k * rows : (k + 1) * rows, z * width : (z + 1) * width] = blocks[
                y_lo, z % zlo, x, y_hi, z // zlo
            ]


def product(weights, flat):
    return lax.dot_general(
        weights[...], flat[...], (((1,), (1,)), ((), ())), preferred_element_type=f32
    )


def first_kernel(mine, w_mine, w_other, out, next_weights, flat, here, sems):
    copies = fetch((w_mine, w_other), (here, next_weights), sems)
    flatten(mine, flat)
    half = len(copies) // 2
    for copy in copies[:half]:
        copy.wait()
    out[...] = product(here, flat)
    for copy in copies[half:]:
        copy.wait()


def second_kernel(place, part, other, weights, kept, sent, flat):
    flatten(other, flat)
    total = part[...] + product(weights, flat)
    half = kept.shape[1]

    @pl.when(place[0] == 0)
    def _():
        kept[...] = total[:, :half]
        sent[...] = total[:, half:]

    @pl.when(place[0] == 1)
    def _():
        kept[...] = total[:, half:]
        sent[...] = total[:, :half]


def stats_kernel(place, kept, got, out):
    def write(policy, refer):
        mixed = (1.0 - BETA) * policy + BETA * refer
        top = jnp.max(policy, 0, keepdims=True)
        mixed_top = jnp.max(mixed, 0, keepdims=True)
        weight = jnp.exp(policy - top)
        total = jnp.sum(weight, 0, keepdims=True)
        cross = jnp.sum(weight * (policy - mixed), 0, keepdims=True) / total
        mixed_total = jnp.sum(jnp.exp(mixed - mixed_top), 0, keepdims=True)
        lines = (top + jnp.log(total), cross, mixed_top + jnp.log(mixed_total))
        out[...] = spread(lines, out.shape)

    @pl.when(place[0] == 0)
    def _():
        write(kept[...], got[...])

    @pl.when(place[0] == 1)
    def _():
        write(got[...], kept[...])


def spread(lines, shape):
    count, height, width = shape
    tail = jnp.zeros((height - len(lines), width), f32)
    tile = jnp.concatenate([*lines, tail], 0)
    return jnp.broadcast_to(tile[None], shape)


def merged(tiles):
    top = jnp.max(tiles, 0)
    weight = jnp.exp(tiles - top[None])
    total = jnp.sum(weight, 0)
    lse = top + jnp.log(total)
    cross = jnp.sum(weight[:, 0:1] * tiles[:, 1:2], 0) / total[0:1]
    return lse[0:1], cross, lse[2:3]


def merge_kernel(tiles, out):
    out[...] = spread(merged(tiles[...]), out.shape)


def final_kernel(tiles, out):
    half = tiles.shape[3]
    for k in range(2):
        policy_lse, cross, mixture_lse = merged(tiles[k])
        lines = (policy_lse, cross - policy_lse + mixture_lse, mixture_lse)
        out[:, k * half : (k + 1) * half] = spread(lines, (1, 8, half))[0]


def sent_kernel(
    place, kept, got, sent, late, final, ids, kl_weight, advantage, w_other,
    turned, sent_out, flat, here, sems,
):
    copies = fetch((w_other,), (here,), sems)
    columns, half = kept.shape
    padded = flat.shape[0]

    def fill(low, high, policy_head):
        for k, (own_ref, partner_ref) in enumerate((low, high)):
            at = slice(k * half, (k + 1) * half)
            policy_lse, divergence, mixture_lse = (final[i : i + 1, at] for i in range(3))
            kl = kl_weight[:, at]
            adv = advantage[:, at]
            token = ids[:, at] - place[2]

            def rows(i, _, own_ref=own_ref, partner_ref=partner_ref):
                start = pl.multiple_of(i * STEP, STEP)
                own, partner = own_ref[pl.ds(start, STEP)], partner_ref[pl.ds(start, STEP)]
                policy, refer = (own, partner) if policy_head else (partner, own)
                mixed = (1.0 - BETA) * policy + BETA * refer
                policy_prob = jnp.exp(policy - policy_lse)
                mixture_prob = jnp.exp(mixed - mixture_lse)
                shift = mixture_prob - policy_prob
                if policy_head:
                    gap = policy - policy_lse - mixed + mixture_lse
                    column = start + lax.broadcasted_iota(jnp.int32, (STEP, half), 0)
                    chosen = (token == column).astype(f32)
                    grad = kl * (
                        policy_prob * (gap - divergence) + (1.0 - BETA) * shift
                    ) - adv * (chosen - policy_prob)
                else:
                    grad = BETA * kl * shift
                flat[pl.ds(start, STEP), at] = grad
                return _

            lax.fori_loop(0, columns // STEP, rows, None, unroll=True)
        flat[columns:, :] = jnp.zeros((padded - columns, flat.shape[1]), f32)
        for start in range(0, padded, LANES):
            turned[:, start : start + LANES] = flat[start : start + LANES, :].T.astype(bf16)

    @pl.when(place[0] == 0)
    def _():
        fill((kept, got), (sent, late), True)

    @pl.when(place[0] == 1)
    def _():
        fill((sent, late), (kept, got), False)

    for copy in copies:
        copy.wait()
    for at, part in sums(turned, here):
        sent_out[:, at] = part.astype(bf16)


def sums(turned, weights, step=512):
    columns, features = weights.shape
    grad = turned[:, :columns]
    for start in range(0, features, step):
        at = slice(start, start + step)
        yield at, lax.dot_general(
            grad, weights[:, at], (((1,), (0,)), ((), ())), preferred_element_type=f32
        )


def own_kernel(turned, w_mine, out, here, sems):
    copies = fetch((w_mine,), (here,), sems)
    for copy in copies:
        copy.wait()
    for at, part in sums(turned, here):
        out[:, at] = part


def pair_kernel(partial, back, out):
    ylo, zlo, xlo, yhi, zhi, rows, width = out.shape
    for z in range(zhi * zlo):
        at = slice(z * width, (z + 1) * width)
        whole = (partial[:, at] + back[:, at].astype(f32)).astype(bf16)
        whole = whole.reshape(xlo, yhi, ylo, rows, width)
        for lo in range(ylo):
            out[lo, z % zlo, :, :, z // zlo] = whole[:, :, lo]


def on_core(kernel, out_shape, count, name, scalars=True, scratch=(), hbm=0):
    return pl.pallas_call(
        kernel,
        in_specs=[SMEM] * scalars + [VMEM] * count + [ANY] * hbm,
        out_specs=jax.tree.map(lambda _: VMEM, out_shape),
        out_shape=out_shape,
        scratch_shapes=scratch,
        compiler_params=(PARAMS, WIDER_PARAMS, WIDE_PARAMS)[hbm],
        name=name,
    )


def array(shape, dtype=f32):
    return jax.ShapeDtypeStruct(shape, dtype)


def neighbours():
    y_count, z_count, cores = (lax.axis_size(axes) for axes in (Y, Z, CORE))

    def pairs(count, core):
        for low in range(0, count, 2):
            yield ((low + 2 * core) % count, low + 1)

    return [
        [(y * z_count + z) * cores + core for y in y_pair for z in z_pair]
        for core in range(cores)
        for y_pair in pairs(y_count, core)
        for z_pair in pairs(z_count, core)
    ]


def swapped_near(parts):
    return lax.all_to_all(
        parts, (*Y, *Z, CORE), 0, 0, axis_index_groups=neighbours(), tiled=True
    )


def swapped_far(parts):
    return lax.all_to_all(parts, FAR, 0, 0, tiled=True)


def repeated(block, count):
    return jnp.broadcast_to(block[None], (count, *block.shape))


def body(hidden, head_weights, token_ids, kl_weight, advantage):
    rows, width = hidden.shape
    columns = head_weights.shape[1]
    xlo, yhi, ylo, zhi, zlo = (lax.axis_size(a) for a in (XLO, YHI, YLO, ZHI, ZLO))
    depth = zhi * zlo
    row_total = rows * xlo * yhi * ylo
    half = row_total // 2
    col_start = lax.axis_index((XLO, *Y, *Z, CORE)) * columns
    place = jnp.stack([lax.axis_index(HEAD), lax.axis_index(CORE), col_start]).astype(jnp.int32)
    w_mine, w_other = held(place, head_weights.T, depth)
    flat = [pltpu.VMEM((row_total, depth * width), bf16)]

    squares = ylo * zlo
    far = swapped_far(repeated(hidden, lax.axis_size(FAR)))
    far, w_mine, w_other = lax.optimization_barrier((far, w_mine, w_other))
    mine = swapped_near(repeated(far, squares).reshape(-1, rows, width))
    other = lax.ppermute(mine, CORE, SWAP)
    shape = (ylo, zlo, xlo, yhi, zhi, rows, width)
    w_half = array((columns, depth * width), bf16)
    buffers = [pltpu.VMEM(w_half.shape, bf16), pltpu.SemaphoreType.DMA((8,))]
    part, w_next = on_core(
        first_kernel,
        [array((columns, row_total)), w_half],
        1,
        "first",
        False,
        scratch=flat + buffers,
        hbm=2,
    )(mine.reshape(shape), w_mine, w_other)
    kept, sent = on_core(
        second_kernel, [array((columns, half))] * 2, 3, "second", scratch=flat
    )(place, part, other.reshape(shape), w_next)

    got = lax.ppermute(sent, HEAD, SWAP)
    near, far = lax.axis_size(STATS_NEAR), lax.axis_size(STATS_FAR)
    stats = on_core(stats_kernel, array((near, 8, half)), 2, "stats")(place, kept, got)
    kept_late, stats = lax.optimization_barrier((kept, stats))
    late = lax.ppermute(kept_late, HEAD, SWAP)
    stats = lax.all_to_all(stats, STATS_NEAR, 0, 0, tiled=True)
    stats = on_core(merge_kernel, array((far, 8, half)), 1, "merge", False)(stats)
    stats = lax.all_to_all(stats, STATS_FAR, 0, 0, tiled=True).reshape(2, far // 2, 8, half)
    final = on_core(final_kernel, array((8, row_total)), 1, "final", False)(stats)

    line = lambda a: a.reshape(1, row_total)
    padded = -(-columns // LANES) * LANES
    wide_rows = (row_total, depth * width)
    turned, sent_part = on_core(
        sent_kernel,
        [array((row_total, padded), bf16), array(wide_rows, bf16)],
        8,
        "sent_part",
        scratch=[pltpu.VMEM((padded, row_total), f32), *buffers],
        hbm=1,
    )(
        place, kept, got, sent, late, final, line(token_ids), line(kl_weight), line(advantage),
        w_other,
    )
    back = lax.ppermute(sent_part, CORE, SWAP)
    partial = on_core(own_kernel, array(wide_rows), 1, "own", False, scratch=buffers, hbm=1)(
        turned, w_mine
    )
    pair_sum = on_core(
        pair_kernel, array(shape, bf16), 2, "pair_sum", False
    )(partial, back)
    near = swapped_near(pair_sum.reshape(-1, rows, width)).reshape(squares, -1, rows, width)
    near = jnp.sum(near.astype(f32), 0).astype(bf16)
    hidden_grad = jnp.sum(swapped_far(near).astype(f32), 0).T
    return (hidden_grad, final[2], final[1])


def solution(mesh):
    finer = Mesh(mesh.devices.reshape(2, 2, 4, 2, 4, 2, 2), (*WIDE, *NARROW))
    return jax.shard_map(
        body,
        mesh=finer,
        in_specs=(P(WIDE, NARROW), P(None, (*WIDE, *NARROW)), P(), P(), P()),
        out_specs=(P(NARROW, WIDE), P(), P()),
        check_vma=False,
    )
```

```python
import jax
import jax.numpy as jnp
from jax import lax
from jax.experimental import pallas as pl
from jax.experimental.pallas import tpu as pltpu
from jax.sharding import Mesh
from jax.sharding import PartitionSpec as P

HEAD, XLO, YHI, YLO, ZHI, ZLO, CORE = "head", "xlo", "yhi", "ylo", "zhi", "zlo", "core"
Y = (YHI, YLO)
Z = (ZHI, ZLO)
NARROW = (*Z, CORE)
WIDE = (HEAD, XLO, *Y)
FAR = (XLO, YHI, ZHI)
STATS_NEAR, STATS_FAR = (*Y, CORE), (HEAD, XLO, *Z)

BETA = 0.2
SWAP = [(0, 1), (1, 0)]
LANES = 128
STEP = 16
f32 = jnp.float32
bf16 = jnp.bfloat16
ANY = pl.BlockSpec(memory_space=pl.ANY)
VMEM = pl.BlockSpec(memory_space=pltpu.VMEM)
SMEM = pl.BlockSpec(memory_space=pltpu.SMEM)
WIDE_PARAMS = pltpu.CompilerParams(vmem_limit_bytes=48 << 20)
WIDER_PARAMS = pltpu.CompilerParams(vmem_limit_bytes=50 << 20)
PARAMS = pltpu.CompilerParams(vmem_limit_bytes=16 << 20)


def hold_kernel(place, weights, mine, other, sems):
    depth = sems.shape[1]
    width = mine.shape[1] // depth
    copies = []
    for side, out in enumerate((mine, other)):
        core = place[1] if side == 0 else 1 - place[1]
        for z in range(depth):
            start = pl.multiple_of((2 * z + core) * width, width)
            source = weights.at[:, pl.ds(start, width)]
            target = out.at[:, z * width : (z + 1) * width]
            copies.append(pltpu.make_async_copy(source, target, sems.at[side, z]))
            copies[-1].start()
    for copy in copies:
        copy.wait()


def held(place, weights, depth):
    columns, features = weights.shape
    half = pltpu.HBM((columns, features // 2), weights.dtype)
    return pl.pallas_call(
        hold_kernel,
        in_specs=[SMEM, ANY],
        out_specs=[ANY, ANY],
        out_shape=[half, half],
        scratch_shapes=[pltpu.SemaphoreType.DMA((2, depth))],
        compiler_params=PARAMS,
        name="hold",
    )(place, weights)


def fetch(sources, targets, sems, pieces=4):
    copies = []
    for k, (source, target) in enumerate(zip(sources, targets)):
        tiles = source.shape[0] // STEP
        for piece in range(pieces):
            low, high = (STEP * (tiles * i // pieces) for i in (piece, piece + 1))
            copies.append(
                pltpu.make_async_copy(
                    source.at[low:high], target.at[low:high], sems.at[k * pieces + piece]
                )
            )
    for copy in copies:
        copy.start()
    return copies


def flatten(blocks, flat):
    ylo, zlo, xlo, yhi, zhi, rows, width = blocks.shape
    for k in range(xlo * yhi * ylo):
        x, y_hi, y_lo = k // (yhi * ylo), k // ylo % yhi, k % ylo
        for z in range(zhi * zlo):
            flat[k * rows : (k + 1) * rows, z * width : (z + 1) * width] = blocks[
                y_lo, z % zlo, x, y_hi, z // zlo
            ]


def product(weights, flat):
    return lax.dot_general(
        weights[...], flat[...], (((1,), (1,)), ((), ())), preferred_element_type=f32
    )


def first_kernel(mine, w_mine, w_other, out, next_weights, flat, here, sems):
    copies = fetch((w_mine, w_other), (here, next_weights), sems)
    flatten(mine, flat)
    half = len(copies) // 2
    for copy in copies[:half]:
        copy.wait()
    out[...] = product(here, flat)
    for copy in copies[half:]:
        copy.wait()


def second_kernel(place, part, other, weights, kept, sent, flat):
    flatten(other, flat)
    total = part[...] + product(weights, flat)
    half = kept.shape[1]

    @pl.when(place[0] == 0)
    def _():
        kept[...] = total[:, :half]
        sent[...] = total[:, half:]

    @pl.when(place[0] == 1)
    def _():
        kept[...] = total[:, half:]
        sent[...] = total[:, :half]


def stats_kernel(place, kept, got, out):
    def write(policy, refer):
        mixed = (1.0 - BETA) * policy + BETA * refer
        top = jnp.max(policy, 0, keepdims=True)
        mixed_top = jnp.max(mixed, 0, keepdims=True)
        weight = jnp.exp(policy - top)
        total = jnp.sum(weight, 0, keepdims=True)
        cross = jnp.sum(weight * (policy - mixed), 0, keepdims=True) / total
        mixed_total = jnp.sum(jnp.exp(mixed - mixed_top), 0, keepdims=True)
        lines = (top + jnp.log(total), cross, mixed_top + jnp.log(mixed_total))
        out[...] = spread(lines, out.shape)

    @pl.when(place[0] == 0)
    def _():
        write(kept[...], got[...])

    @pl.when(place[0] == 1)
    def _():
        write(got[...], kept[...])


def spread(lines, shape):
    count, height, width = shape
    tail = jnp.zeros((height - len(lines), width), f32)
    tile = jnp.concatenate([*lines, tail], 0)
    return jnp.broadcast_to(tile[None], shape)


def merged(tiles):
    top = jnp.max(tiles, 0)
    weight = jnp.exp(tiles - top[None])
    total = jnp.sum(weight, 0)
    lse = top + jnp.log(total)
    cross = jnp.sum(weight[:, 0:1] * tiles[:, 1:2], 0) / total[0:1]
    return lse[0:1], cross, lse[2:3]


def merge_kernel(tiles, out):
    out[...] = spread(merged(tiles[...]), out.shape)


def final_kernel(tiles, out, lse_out, divergence_out):
    half = tiles.shape[3]
    for k in range(2):
        policy_lse, cross, mixture_lse = merged(tiles[k])
        divergence = cross - policy_lse + mixture_lse
        at = slice(k * half, (k + 1) * half)
        out[:, at] = spread((policy_lse, divergence, mixture_lse), (1, 8, half))[0]
        lse_out[:, at] = mixture_lse
        divergence_out[:, at] = divergence


def sent_kernel(
    place, kept, got, sent, late, final, ids, kl_weight, advantage, w_other,
    turned, sent_out, flat, here, sems,
):
    copies = fetch((w_other,), (here,), sems)
    columns, half = kept.shape
    padded = flat.shape[0]

    def fill(low, high, policy_head):
        for k, (own_ref, partner_ref) in enumerate((low, high)):
            at = slice(k * half, (k + 1) * half)
            policy_lse, divergence, mixture_lse = (final[i : i + 1, at] for i in range(3))
            kl = kl_weight[:, at]
            adv = advantage[:, at]
            token = ids[:, at] - place[2]

            def rows(i, _, own_ref=own_ref, partner_ref=partner_ref):
                start = pl.multiple_of(i * STEP, STEP)
                own, partner = own_ref[pl.ds(start, STEP)], partner_ref[pl.ds(start, STEP)]
                policy, refer = (own, partner) if policy_head else (partner, own)
                mixed = (1.0 - BETA) * policy + BETA * refer
                policy_prob = jnp.exp(policy - policy_lse)
                mixture_prob = jnp.exp(mixed - mixture_lse)
                shift = mixture_prob - policy_prob
                if policy_head:
                    gap = policy - policy_lse - mixed + mixture_lse
                    column = start + lax.broadcasted_iota(jnp.int32, (STEP, half), 0)
                    chosen = (token == column).astype(f32)
                    grad = kl * (
                        policy_prob * (gap - divergence) + (1.0 - BETA) * shift
                    ) - adv * (chosen - policy_prob)
                else:
                    grad = BETA * kl * shift
                flat[pl.ds(start, STEP), at] = grad
                return _

            lax.fori_loop(0, columns // STEP, rows, None, unroll=True)
        flat[columns:, :] = jnp.zeros((padded - columns, flat.shape[1]), f32)
        for start in range(0, padded, LANES):
            turned[:, start : start + LANES] = flat[start : start + LANES, :].T.astype(bf16)

    @pl.when(place[0] == 0)
    def _():
        fill((kept, got), (sent, late), True)

    @pl.when(place[0] == 1)
    def _():
        fill((sent, late), (kept, got), False)

    for copy in copies:
        copy.wait()
    for at, part in sums(turned, here):
        sent_out[:, at] = part.astype(bf16)


def sums(turned, weights, step=512):
    columns, features = weights.shape
    grad = turned[:, :columns]
    for start in range(0, features, step):
        at = slice(start, start + step)
        yield at, lax.dot_general(
            grad, weights[:, at], (((1,), (0,)), ((), ())), preferred_element_type=f32
        )


def own_kernel(turned, w_mine, out, here, sems):
    copies = fetch((w_mine,), (here,), sems)
    for copy in copies:
        copy.wait()
    for at, part in sums(turned, here):
        out[:, at] = part


def pair_kernel(partial, back, out):
    ylo, zlo, xlo, yhi, zhi, rows, width = out.shape
    for z in range(zhi * zlo):
        at = slice(z * width, (z + 1) * width)
        whole = (partial[:, at] + back[:, at].astype(f32)).astype(bf16)
        whole = whole.reshape(xlo, yhi, ylo, rows, width)
        for lo in range(ylo):
            out[lo, z % zlo, :, :, z // zlo] = whole[:, :, lo]


def on_core(kernel, out_shape, count, name, scalars=True, scratch=(), hbm=0):
    return pl.pallas_call(
        kernel,
        in_specs=[SMEM] * scalars + [VMEM] * count + [ANY] * hbm,
        out_specs=jax.tree.map(lambda _: VMEM, out_shape),
        out_shape=out_shape,
        scratch_shapes=scratch,
        compiler_params=(PARAMS, WIDER_PARAMS, WIDE_PARAMS)[hbm],
        name=name,
    )


def array(shape, dtype=f32):
    return jax.ShapeDtypeStruct(shape, dtype)


def neighbours():
    y_count, z_count, cores = (lax.axis_size(axes) for axes in (Y, Z, CORE))

    def pairs(count, core):
        for low in range(0, count, 2):
            yield ((low + 2 * core) % count, low + 1)

    return [
        [(y * z_count + z) * cores + core for y in y_pair for z in z_pair]
        for core in range(cores)
        for y_pair in pairs(y_count, core)
        for z_pair in pairs(z_count, core)
    ]


def swapped_near(parts):
    return lax.all_to_all(
        parts, (*Y, *Z, CORE), 0, 0, axis_index_groups=neighbours(), tiled=True
    )


def swapped_far(parts):
    return lax.all_to_all(parts, FAR, 0, 0, tiled=True)


def repeated(block, count):
    return jnp.broadcast_to(block[None], (count, *block.shape))


def body(hidden, head_weights, token_ids, kl_weight, advantage):
    rows, width = hidden.shape
    columns = head_weights.shape[1]
    xlo, yhi, ylo, zhi, zlo = (lax.axis_size(a) for a in (XLO, YHI, YLO, ZHI, ZLO))
    depth = zhi * zlo
    row_total = rows * xlo * yhi * ylo
    half = row_total // 2
    col_start = lax.axis_index((XLO, *Y, *Z, CORE)) * columns
    place = jnp.stack([lax.axis_index(HEAD), lax.axis_index(CORE), col_start]).astype(jnp.int32)
    w_mine, w_other = held(place, head_weights.T, depth)
    flat = [pltpu.VMEM((row_total, depth * width), bf16)]

    squares = ylo * zlo
    far = swapped_far(repeated(hidden, lax.axis_size(FAR)))
    far, w_mine, w_other = lax.optimization_barrier((far, w_mine, w_other))
    mine = swapped_near(repeated(far, squares).reshape(-1, rows, width))
    other = lax.ppermute(mine, CORE, SWAP)
    shape = (ylo, zlo, xlo, yhi, zhi, rows, width)
    w_half = array((columns, depth * width), bf16)
    buffers = [pltpu.VMEM(w_half.shape, bf16), pltpu.SemaphoreType.DMA((8,))]
    part, w_next = on_core(
        first_kernel,
        [array((columns, row_total)), w_half],
        1,
        "first",
        False,
        scratch=flat + buffers,
        hbm=2,
    )(mine.reshape(shape), w_mine, w_other)
    kept, sent = on_core(
        second_kernel, [array((columns, half))] * 2, 3, "second", scratch=flat
    )(place, part, other.reshape(shape), w_next)

    got = lax.ppermute(sent, HEAD, SWAP)
    near, far = lax.axis_size(STATS_NEAR), lax.axis_size(STATS_FAR)
    stats = on_core(stats_kernel, array((near, 8, half)), 2, "stats")(place, kept, got)
    kept_late, stats = lax.optimization_barrier((kept, stats))
    late = lax.ppermute(kept_late, HEAD, SWAP)
    stats = lax.all_to_all(stats, STATS_NEAR, 0, 0, tiled=True)
    stats = on_core(merge_kernel, array((far, 8, half)), 1, "merge", False)(stats)
    stats = lax.all_to_all(stats, STATS_FAR, 0, 0, tiled=True).reshape(2, far // 2, 8, half)
    final, mixture_lse, divergence = on_core(
        final_kernel, [array((n, row_total)) for n in (8, 1, 1)], 1, "final", False
    )(stats)

    line = lambda a: a.reshape(1, row_total)
    padded = -(-columns // LANES) * LANES
    wide_rows = (row_total, depth * width)
    turned, sent_part = on_core(
        sent_kernel,
        [array((row_total, padded), bf16), array(wide_rows, bf16)],
        8,
        "sent_part",
        scratch=[pltpu.VMEM((padded, row_total), f32), *buffers],
        hbm=1,
    )(
        place, kept, got, sent, late, final, line(token_ids), line(kl_weight), line(advantage),
        w_other,
    )
    back = lax.ppermute(sent_part, CORE, SWAP)
    partial = on_core(own_kernel, array(wide_rows), 1, "own", False, scratch=buffers, hbm=1)(
        turned, w_mine
    )
    pair_sum = on_core(
        pair_kernel, array(shape, bf16), 2, "pair_sum", False
    )(partial, back)
    near = swapped_near(pair_sum.reshape(-1, rows, width)).reshape(squares, -1, rows, width)
    near = jnp.sum(near.astype(f32), 0).astype(bf16)
    hidden_grad = jnp.sum(swapped_far(near).astype(f32), 0).T
    return (hidden_grad, mixture_lse.reshape(row_total), divergence.reshape(row_total))


def solution(mesh):
    finer = Mesh(mesh.devices.reshape(2, 2, 4, 2, 4, 2, 2), (*WIDE, *NARROW))
    return jax.shard_map(
        body,
        mesh=finer,
        in_specs=(P(WIDE, NARROW), P(None, (*WIDE, *NARROW)), P(), P(), P()),
        out_specs=(P(NARROW, WIDE), P(), P()),
        check_vma=False,
    )
```

```python
import jax
import jax.numpy as jnp
from jax import lax
from jax.experimental import pallas as pl
from jax.experimental.pallas import tpu as pltpu
from jax.sharding import Mesh
from jax.sharding import PartitionSpec as P

HEAD, XLO, YHI, YLO, ZHI, ZLO, CORE = "head", "xlo", "yhi", "ylo", "zhi", "zlo", "core"
Y = (YHI, YLO)
Z = (ZHI, ZLO)
NARROW = (*Z, CORE)
WIDE = (HEAD, XLO, *Y)
FAR = (XLO, YHI, ZHI)
STATS_NEAR, STATS_FAR = (*Y, CORE), (HEAD, XLO, *Z)

BETA = 0.2
SWAP = [(0, 1), (1, 0)]
LANES = 128
STEP = 16
f32 = jnp.float32
bf16 = jnp.bfloat16
ANY = pl.BlockSpec(memory_space=pl.ANY)
VMEM = pl.BlockSpec(memory_space=pltpu.VMEM)
SMEM = pl.BlockSpec(memory_space=pltpu.SMEM)
WIDE_PARAMS = pltpu.CompilerParams(vmem_limit_bytes=48 << 20)
WIDER_PARAMS = pltpu.CompilerParams(vmem_limit_bytes=50 << 20)
PARAMS = pltpu.CompilerParams(vmem_limit_bytes=16 << 20)


def hold_kernel(place, weights, mine, other, sems):
    depth = sems.shape[1]
    width = mine.shape[1] // depth
    copies = []
    for side, out in enumerate((mine, other)):
        core = place[1] if side == 0 else 1 - place[1]
        for z in range(depth):
            start = pl.multiple_of((2 * z + core) * width, width)
            source = weights.at[:, pl.ds(start, width)]
            target = out.at[:, z * width : (z + 1) * width]
            copies.append(pltpu.make_async_copy(source, target, sems.at[side, z]))
            copies[-1].start()
    for copy in copies:
        copy.wait()


def held(place, weights, depth):
    columns, features = weights.shape
    half = pltpu.HBM((columns, features // 2), weights.dtype)
    return pl.pallas_call(
        hold_kernel,
        in_specs=[SMEM, ANY],
        out_specs=[ANY, ANY],
        out_shape=[half, half],
        scratch_shapes=[pltpu.SemaphoreType.DMA((2, depth))],
        compiler_params=PARAMS,
        name="hold",
    )(place, weights)


def fetch(sources, targets, sems, pieces=4):
    copies = []
    for k, (source, target) in enumerate(zip(sources, targets)):
        tiles = source.shape[0] // STEP
        for piece in range(pieces):
            low, high = (STEP * (tiles * i // pieces) for i in (piece, piece + 1))
            copies.append(
                pltpu.make_async_copy(
                    source.at[low:high], target.at[low:high], sems.at[k * pieces + piece]
                )
            )
    for copy in copies:
        copy.start()
    return copies


def flatten(blocks, flat):
    ylo, zlo, xlo, yhi, zhi, rows, width = blocks.shape
    for k in range(xlo * yhi * ylo):
        x, y_hi, y_lo = k // (yhi * ylo), k // ylo % yhi, k % ylo
        for z in range(zhi * zlo):
            flat[k * rows : (k + 1) * rows, z * width : (z + 1) * width] = blocks[
                y_lo, z % zlo, x, y_hi, z // zlo
            ]


def product(weights, flat):
    return lax.dot_general(
        weights[...], flat[...], (((1,), (1,)), ((), ())), preferred_element_type=f32
    )


def first_kernel(mine, w_mine, w_other, out, next_weights, flat, here, sems):
    copies = fetch((w_mine, w_other), (here, next_weights), sems)
    flatten(mine, flat)
    half = len(copies) // 2
    for copy in copies[:half]:
        copy.wait()
    out[...] = product(here, flat)
    for copy in copies[half:]:
        copy.wait()


def second_kernel(place, part, other, weights, kept, sent, flat):
    flatten(other, flat)
    total = part[...] + product(weights, flat)
    half = kept.shape[1]

    @pl.when(place[0] == 0)
    def _():
        kept[...] = total[:, :half]
        sent[...] = total[:, half:]

    @pl.when(place[0] == 1)
    def _():
        kept[...] = total[:, half:]
        sent[...] = total[:, :half]


def stats_kernel(place, kept, got, out):
    def write(policy, refer):
        mixed = (1.0 - BETA) * policy + BETA * refer
        top = jnp.max(policy, 0, keepdims=True)
        mixed_top = jnp.max(mixed, 0, keepdims=True)
        weight = jnp.exp(policy - top)
        total = jnp.sum(weight, 0, keepdims=True)
        cross = jnp.sum(weight * (policy - mixed), 0, keepdims=True) / total
        mixed_total = jnp.sum(jnp.exp(mixed - mixed_top), 0, keepdims=True)
        lines = (top + jnp.log(total), cross, mixed_top + jnp.log(mixed_total))
        out[...] = spread(lines, out.shape)

    @pl.when(place[0] == 0)
    def _():
        write(kept[...], got[...])

    @pl.when(place[0] == 1)
    def _():
        write(got[...], kept[...])


def spread(lines, shape):
    count, height, width = shape
    tail = jnp.zeros((height - len(lines), width), f32)
    tile = jnp.concatenate([*lines, tail], 0)
    return jnp.broadcast_to(tile[None], shape)


def merged(tiles):
    top = jnp.max(tiles, 0)
    weight = jnp.exp(tiles - top[None])
    total = jnp.sum(weight, 0)
    lse = top + jnp.log(total)
    cross = jnp.sum(weight[:, 0:1] * tiles[:, 1:2], 0) / total[0:1]
    return lse[0:1], cross, lse[2:3]


def merge_kernel(tiles, out):
    out[...] = spread(merged(tiles[...]), out.shape)


def final_kernel(tiles, out, lse_out, divergence_out):
    half = tiles.shape[3]
    for k in range(2):
        policy_lse, cross, mixture_lse = merged(tiles[k])
        divergence = cross - policy_lse + mixture_lse
        at = slice(k * half, (k + 1) * half)
        out[:, at] = spread((policy_lse, divergence, mixture_lse), (1, 8, half))[0]
        lse_out[:, at] = mixture_lse
        divergence_out[:, at] = divergence


def sent_kernel(
    place, kept, got, sent, late, final, ids, kl_weight, advantage, w_other,
    turned, sent_out, flat,
):
    columns, half = kept.shape
    padded = flat.shape[0]

    def fill(low, high, policy_head):
        for k, (own_ref, partner_ref) in enumerate((low, high)):
            at = slice(k * half, (k + 1) * half)
            policy_lse, divergence, mixture_lse = (final[i : i + 1, at] for i in range(3))
            kl = kl_weight[:, at]
            adv = advantage[:, at]
            token = ids[:, at] - place[2]

            def rows(i, _, own_ref=own_ref, partner_ref=partner_ref):
                start = pl.multiple_of(i * STEP, STEP)
                own, partner = own_ref[pl.ds(start, STEP)], partner_ref[pl.ds(start, STEP)]
                policy, refer = (own, partner) if policy_head else (partner, own)
                mixed = (1.0 - BETA) * policy + BETA * refer
                policy_prob = jnp.exp(policy - policy_lse)
                mixture_prob = jnp.exp(mixed - mixture_lse)
                shift = mixture_prob - policy_prob
                if policy_head:
                    gap = policy - policy_lse - mixed + mixture_lse
                    column = start + lax.broadcasted_iota(jnp.int32, (STEP, half), 0)
                    chosen = (token == column).astype(f32)
                    grad = kl * (
                        policy_prob * (gap - divergence) + (1.0 - BETA) * shift
                    ) - adv * (chosen - policy_prob)
                else:
                    grad = BETA * kl * shift
                flat[pl.ds(start, STEP), at] = grad
                return _

            lax.fori_loop(0, columns // STEP, rows, None, unroll=True)
        flat[columns:, :] = jnp.zeros((padded - columns, flat.shape[1]), f32)
        for start in range(0, padded, LANES):
            turned[:, start : start + LANES] = flat[start : start + LANES, :].T.astype(bf16)

    @pl.when(place[0] == 0)
    def _():
        fill((kept, got), (sent, late), True)

    @pl.when(place[0] == 1)
    def _():
        fill((sent, late), (kept, got), False)

    for at, part in sums(turned, w_other):
        sent_out[:, at] = part.astype(bf16)


def fetch_kernel(weights, out, sems):
    for copy in fetch((weights,), (out,), sems):
        copy.wait()


def sums(turned, weights, step=512):
    columns, features = weights.shape
    grad = turned[:, :columns]
    for start in range(0, features, step):
        at = slice(start, start + step)
        yield at, lax.dot_general(
            grad, weights[:, at], (((1,), (0,)), ((), ())), preferred_element_type=f32
        )


def own_kernel(turned, w_mine, out, here, sems):
    copies = fetch((w_mine,), (here,), sems)
    for copy in copies:
        copy.wait()
    for at, part in sums(turned, here):
        out[:, at] = part


def pair_kernel(partial, back, out):
    ylo, zlo, xlo, yhi, zhi, rows, width = out.shape
    for z in range(zhi * zlo):
        at = slice(z * width, (z + 1) * width)
        whole = (partial[:, at] + back[:, at].astype(f32)).astype(bf16)
        whole = whole.reshape(xlo, yhi, ylo, rows, width)
        for lo in range(ylo):
            out[lo, z % zlo, :, :, z // zlo] = whole[:, :, lo]


def on_core(kernel, out_shape, count, name, scalars=True, scratch=(), hbm=0):
    return pl.pallas_call(
        kernel,
        in_specs=[SMEM] * scalars + [VMEM] * count + [ANY] * hbm,
        out_specs=jax.tree.map(lambda _: VMEM, out_shape),
        out_shape=out_shape,
        scratch_shapes=scratch,
        compiler_params=(PARAMS, WIDER_PARAMS, WIDE_PARAMS)[hbm],
        name=name,
    )


def array(shape, dtype=f32):
    return jax.ShapeDtypeStruct(shape, dtype)


def neighbours():
    y_count, z_count, cores = (lax.axis_size(axes) for axes in (Y, Z, CORE))

    def pairs(count, core):
        for low in range(0, count, 2):
            yield ((low + 2 * core) % count, low + 1)

    return [
        [(y * z_count + z) * cores + core for y in y_pair for z in z_pair]
        for core in range(cores)
        for y_pair in pairs(y_count, core)
        for z_pair in pairs(z_count, core)
    ]


def swapped_near(parts):
    return lax.all_to_all(
        parts, (*Y, *Z, CORE), 0, 0, axis_index_groups=neighbours(), tiled=True
    )


def swapped_far(parts):
    return lax.all_to_all(parts, FAR, 0, 0, tiled=True)


def repeated(block, count):
    return jnp.broadcast_to(block[None], (count, *block.shape))


def body(hidden, head_weights, token_ids, kl_weight, advantage):
    rows, width = hidden.shape
    columns = head_weights.shape[1]
    xlo, yhi, ylo, zhi, zlo = (lax.axis_size(a) for a in (XLO, YHI, YLO, ZHI, ZLO))
    depth = zhi * zlo
    row_total = rows * xlo * yhi * ylo
    half = row_total // 2
    col_start = lax.axis_index((XLO, *Y, *Z, CORE)) * columns
    place = jnp.stack([lax.axis_index(HEAD), lax.axis_index(CORE), col_start]).astype(jnp.int32)
    w_mine, w_other = held(place, head_weights.T, depth)
    flat = [pltpu.VMEM((row_total, depth * width), bf16)]

    squares = ylo * zlo
    far = swapped_far(repeated(hidden, lax.axis_size(FAR)))
    far, w_mine, w_other = lax.optimization_barrier((far, w_mine, w_other))
    mine = swapped_near(repeated(far, squares).reshape(-1, rows, width))
    other = lax.ppermute(mine, CORE, SWAP)
    shape = (ylo, zlo, xlo, yhi, zhi, rows, width)
    w_half = array((columns, depth * width), bf16)
    buffers = [pltpu.VMEM(w_half.shape, bf16), pltpu.SemaphoreType.DMA((8,))]
    part, w_next = on_core(
        first_kernel,
        [array((columns, row_total)), w_half],
        1,
        "first",
        False,
        scratch=flat + buffers,
        hbm=2,
    )(mine.reshape(shape), w_mine, w_other)
    kept, sent = on_core(
        second_kernel, [array((columns, half))] * 2, 3, "second", scratch=flat
    )(place, part, other.reshape(shape), w_next)

    got = lax.ppermute(sent, HEAD, SWAP)
    near, far = lax.axis_size(STATS_NEAR), lax.axis_size(STATS_FAR)
    stats = on_core(stats_kernel, array((near, 8, half)), 2, "stats")(place, kept, got)
    kept_late, stats, w_other = lax.optimization_barrier((kept, stats, w_other))
    late = lax.ppermute(kept_late, HEAD, SWAP)
    w_near = on_core(
        fetch_kernel, w_half, 0, "fetch", False, scratch=buffers[1:], hbm=1
    )(w_other)
    stats = lax.all_to_all(stats, STATS_NEAR, 0, 0, tiled=True)
    stats, w_near = lax.optimization_barrier((stats, w_near))
    stats = on_core(merge_kernel, array((far, 8, half)), 1, "merge", False)(stats)
    stats = lax.all_to_all(stats, STATS_FAR, 0, 0, tiled=True).reshape(2, far // 2, 8, half)
    final, mixture_lse, divergence = on_core(
        final_kernel, [array((n, row_total)) for n in (8, 1, 1)], 1, "final", False
    )(stats)

    line = lambda a: a.reshape(1, row_total)
    padded = -(-columns // LANES) * LANES
    wide_rows = (row_total, depth * width)
    turned, sent_part = on_core(
        sent_kernel,
        [array((row_total, padded), bf16), array(wide_rows, bf16)],
        9,
        "sent_part",
        scratch=[pltpu.VMEM((padded, row_total), f32)],
    )(
        place, kept, got, sent, late, final, line(token_ids), line(kl_weight), line(advantage),
        w_near,
    )
    back = lax.ppermute(sent_part, CORE, SWAP)
    partial = on_core(own_kernel, array(wide_rows), 1, "own", False, scratch=buffers, hbm=1)(
        turned, w_mine
    )
    pair_sum = on_core(
        pair_kernel, array(shape, bf16), 2, "pair_sum", False
    )(partial, back)
    near = swapped_near(pair_sum.reshape(-1, rows, width)).reshape(squares, -1, rows, width)
    near = jnp.sum(near.astype(f32), 0).astype(bf16)
    hidden_grad = jnp.sum(swapped_far(near).astype(f32), 0).T
    return (hidden_grad, mixture_lse.reshape(row_total), divergence.reshape(row_total))


def solution(mesh):
    finer = Mesh(mesh.devices.reshape(2, 2, 4, 2, 4, 2, 2), (*WIDE, *NARROW))
    return jax.shard_map(
        body,
        mesh=finer,
        in_specs=(P(WIDE, NARROW), P(None, (*WIDE, *NARROW)), P(), P(), P()),
        out_specs=(P(NARROW, WIDE), P(), P()),
        check_vma=False,
    )
```
